512 devices in a mesh: row: 8 (over y), col: 64 (over z, x, core).
Axes of the slice: x: 4, y: 8, z: 8, core: 2. Of those that a mesh axis runs over, the one named last changes fastest.
Arguments:
- sigma_top: bfloat16 [16384, 8, 64, 32], P('row', None, 'col'), as said below
- ancestor_rows: float32 [16384, 1024], P(('row', 'col')), may hold values from -0.0009765625 to 0.0009765625
- window_rows: float32 [1024, 1024], P('col'), may hold values from -0.1875 to 0.1875
- tile_inverse: float32 [4, 256, 256], replicated, as said below
- structure: int32 [4, 64], replicated, may hold values from 0 to 1, as said below
Outputs:
- cross_covariance: float32 [16384, 1024], P(('row', 'col'))
- window_covariance: float32 [1024, 1024], P('col')
The draws below stay inside these ranges and needn't reach their ends.
Inputs may be any that keep to these rules, and one draw needn't show every extreme that they name: `sigma_top`: symmetric as an 16384 x 16384 matrix. `tile_inverse`: each tile is lower triangular. A tile in the structure of supernode j lies in the structure of every earlier supernode; supernode 0's structure holds every ancestor tile.
All inputs are finite; a program needn't handle non-finite values.
Results may differ from the reference program's by a relative error of at most 0.0013.
The reference program's roundings to bfloat16 on the way count: a program that leaves them out, or rounds other values in their place, can miss the bound.
Values may be sent and summed in bfloat16 or wider, within the bound.
No kernel may reach another device: no remote copies, remote signals or barrier semaphores. Data moves between devices by JAX's collectives and lax.ppermute only.
A program may use at most 64 MiB of HBM per device.

```python
import math
import jax
import jax.numpy as jnp
from jax import lax

B = 256
K = 4
RD_A = 32
MA = 16384
NA = 64
N_ROW = 8
N_COL = 64


def draw_sigma_top(key, part):
    first, second = jax.random.split(key, 2)
    raw = jax.random.normal(first, (MA, MA), jnp.float32)
    symmetric = (raw + raw.T) * (0.7071 / math.sqrt(MA))
    levels = 1.5 + jnp.exp(jax.random.uniform(second, (MA,), jnp.float32, 0.0, math.log(10.0)))
    identity = jnp.arange(MA, dtype=jnp.int32)[:, None] == jnp.arange(MA, dtype=jnp.int32)[None, :]
    matrix = jnp.where(identity, levels[:, None], symmetric)
    return (matrix * float(MA)).reshape(MA, N_ROW, N_COL, RD_A).astype(jnp.bfloat16)


def draw_tile_inverse(key, part):
    first, second = jax.random.split(key, 2)
    lower = jnp.arange(B, dtype=jnp.int32)[:, None] > jnp.arange(B, dtype=jnp.int32)[None, :]
    same = jnp.arange(B, dtype=jnp.int32)[:, None] == jnp.arange(B, dtype=jnp.int32)[None, :]
    entries = jax.random.normal(first, (K, B, B), jnp.float32) * (0.5 / math.sqrt(B))
    levels = jnp.exp(jax.random.uniform(second, (K, B, 1), jnp.float32, math.log(0.5), math.log(2.0)))
    return jnp.where(lower[None], entries, jnp.where(same[None], levels, 0.0))


def draw_structure(key, part):
    depth = jax.random.randint(key, (1, NA), 1, K + 1)
    return (jnp.arange(K, dtype=jnp.int32)[:, None] < depth).astype(jnp.int32)


def block_scale(own_key, shape, pieces, smallest, largest):
    factor_of, own = 1.0, jax.random.fold_in(own_key, 6)
    for dim, parts in pieces:
        draws = jnp.exp(jax.random.uniform(jax.random.fold_in(own, dim), (parts,), jnp.float32, smallest / len(pieces), largest / len(pieces)))
        factor_of = factor_of * jnp.repeat(draws, shape[dim] // parts).reshape([-1 if axis == dim else 1 for axis in range(len(shape))])
    return factor_of


def scatter_about(stream_key, dims, deviation, bound, cuts=(), held_as=jnp.bfloat16):
    level = block_scale(stream_key, dims, cuts, -0.22, 0.18) if cuts else 1.0
    values = jax.random.normal(stream_key, dims, jnp.float32) * deviation * level
    return jnp.minimum(jnp.maximum(values, -bound), bound).astype(held_as)


def setup_inputs(seed: int = 0) -> dict:
    key_list = jax.random.split(jax.random.key(seed), 6)
    sigma_top = draw_sigma_top(jax.random.fold_in(key_list[5], 71), 0)
    ancestor_rows = scatter_about(key_list[1], (MA, K * B), (MA ** -1), 0.0009765625, ((0, 512),), jnp.float32)
    window_rows = scatter_about(key_list[2], (K * B, K * B), (K * B) ** -0.5, 0.1875, ((0, 64),), jnp.float32)
    tile_inverse = draw_tile_inverse(jax.random.fold_in(key_list[5], 71), 0)
    structure = draw_structure(jax.random.fold_in(key_list[5], 71), 0)
    return dict(sigma_top=sigma_top, ancestor_rows=ancestor_rows, window_rows=window_rows, tile_inverse=tile_inverse, structure=structure)


def reference(sigma_top, ancestor_rows, window_rows, tile_inverse, structure):
    highest = lax.Precision.HIGHEST
    whole = sigma_top.reshape(MA, MA)
    window = K * B
    tiles_ancestor = jnp.arange(MA, dtype=jnp.int32) // B
    tiles_window = jnp.arange(window, dtype=jnp.int32) // B
    upper_mask = tiles_window[None, :] > tiles_window[:, None]
    panels_ancestor = []
    panels_window = []
    selections = []
    for supernode in range(K):
        inverse = tile_inverse[supernode]
        select = structure[supernode][tiles_ancestor].astype(jnp.float32)
        selections.append(select)
        product = jnp.dot(ancestor_rows[:, supernode * B:(supernode + 1) * B], inverse, precision=highest, preferred_element_type=jnp.float32)
        panels_ancestor.append((select[:, None] * product).astype(jnp.bfloat16))
        keep = (tiles_window < supernode).astype(jnp.float32)
        product = jnp.dot(window_rows[:, supernode * B:(supernode + 1) * B], inverse, precision=highest, preferred_element_type=jnp.float32)
        panels_window.append((keep[:, None] * product).astype(jnp.bfloat16))
    ancestor_all = jnp.dot(whole, jnp.concatenate(panels_ancestor, axis=1), preferred_element_type=jnp.float32)
    cross = jnp.zeros((MA, window), jnp.float32)
    block = jnp.zeros((window, window), jnp.float32)
    for supernode in range(K):
        left_edge = supernode * B
        right_edge = left_edge + B
        inverse = tile_inverse[supernode]
        select = selections[supernode]
        ancestor_f32 = panels_ancestor[supernode].astype(jnp.float32)
        window_f32 = panels_window[supernode].astype(jnp.float32)
        result_ancestor = select[:, None] * (ancestor_all[:, left_edge:right_edge] + jnp.dot(cross, window_f32, precision=highest, preferred_element_type=jnp.float32))
        upper = jnp.where(upper_mask, block, 0.0)
        result_window = jnp.dot(cross.T, ancestor_f32, precision=highest, preferred_element_type=jnp.float32)
        result_window = result_window + jnp.dot(block.T, window_f32, precision=highest, preferred_element_type=jnp.float32)
        result_window = result_window + jnp.dot(upper, window_f32, precision=highest, preferred_element_type=jnp.float32)
        diagonal = jnp.dot(inverse.T, inverse, precision=highest, preferred_element_type=jnp.float32)
        diagonal = diagonal + jnp.dot(ancestor_f32.T, result_ancestor, precision=highest, preferred_element_type=jnp.float32)
        diagonal = diagonal + jnp.dot(window_f32.T, result_window, precision=highest, preferred_element_type=jnp.float32)
        placed = jnp.zeros((window, B), jnp.float32).at[left_edge:right_edge].set(diagonal)
        row_tiles = tiles_window[:, None]
        column = jnp.where(row_tiles < supernode, -result_window, jnp.where(row_tiles == supernode, placed, 0.0))
        cross = cross.at[:, left_edge:right_edge].set(-result_ancestor)
        block = block.at[:, left_edge:right_edge].set(column)
    return cross, block
```

```python
import jax
import jax.numpy as jnp
from jax import lax
from jax.sharding import Mesh, PartitionSpec as P

HIGHEST = lax.Precision.HIGHEST
HIGH = lax.Precision.HIGH
BF16 = jnp.bfloat16
F32 = jnp.float32


def mm(a, b, precision=HIGH):
    return jnp.dot(a, b, precision=precision, preferred_element_type=F32)


def mm_t(a, b, precision=HIGH):
    return lax.dot_general(
        a, b, (((0,), (0,)), ((), ())), precision=precision, preferred_element_type=F32
    )


def exchange(x, axis):
    return lax.all_to_all(x, axis, 0, 0, tiled=True)


def gather(x, axis, size):
    return exchange(jnp.broadcast_to(x[None], (size,) + x.shape), axis)


def body(sigma_top, ancestor_rows, window_rows, tile_inverse, structure):
    ny, nz, nx, nc = 8, 8, 4, 2
    supernodes, width = tile_inverse.shape[0], tile_inverse.shape[1]
    window = supernodes * width
    local = ancestor_rows.shape[0]
    wlocal = window_rows.shape[0]
    y, z, x, c = (lax.axis_index(name) for name in ("y", "z", "x", "c"))
    col = (z * nx + x) * nc + c
    tile = ((y * (nz * nx * nc) + col) * local) // width
    wtile = (col * wlocal) // width
    select = lax.dynamic_slice_in_dim(structure, tile, 1, 1)[:, 0].astype(F32)

    with jax.named_scope("panels"):
        rows = jnp.concatenate([ancestor_rows, window_rows], axis=0)
        pieces = [
            mm(rows[:, j * width : (j + 1) * width], tile_inverse[j], HIGHEST)
            for j in range(supernodes)
        ]
        panel = jnp.concatenate(
            [(select[j] * pieces[j][:local]).astype(BF16) for j in range(supernodes)], axis=1
        )
        wpanel = jnp.concatenate(
            [
                ((wtile < j).astype(F32) * pieces[j][local:]).astype(BF16)
                for j in range(1, supernodes)
            ],
            axis=1,
        )
        half = window - width
        folded = jnp.concatenate([wpanel[:, : half // 2], wpanel[:, half // 2 :]], axis=0)
        message = jnp.concatenate([panel, folded], axis=1)

    with jax.named_scope("column_block"):
        doubled = jnp.concatenate([panel, panel], axis=1)
        panel_c = lax.all_gather(doubled, "y", axis=0, tiled=True)[:, :window]

    with jax.named_scope("sigma"):
        sigma = sigma_top.reshape(nz, nx, nc, local, ny * local)
        mine = lax.dynamic_index_in_dim(sigma, c, 2, keepdims=False)
        other = lax.dynamic_index_in_dim(sigma, 1 - c, 2, keepdims=False)
        mine = mine.transpose(1, 0, 2, 3).reshape(-1, ny * local)
        other = other.transpose(1, 0, 2, 3).reshape(-1, ny * local)

    with jax.named_scope("gather"):
        got = gather(message, "z", nz).reshape(nz * local, -1)
        got = gather(got, "x", nx).reshape(nx * nz * local, -1)
        sibling = lax.ppermute(got, "c", [(0, 1), (1, 0)])
        product = mm_t(mine, got[:, :window], None) + mm_t(other, sibling[:, :window], None)

    with jax.named_scope("unit_inverse"):
        swap = c == 1
        w_mine, w_other = (
            v[:, window:].reshape(nx, nz, 2, wlocal, half // 2) for v in (got, sibling)
        )
        w_all = jnp.stack(
            [jnp.where(swap, w_other, w_mine), jnp.where(swap, w_mine, w_other)], axis=0
        )
        w_all = w_all.transpose(2, 1, 0, 3, 4, 5)
        w_all = jnp.concatenate([w_all[:, :, :, 0], w_all[:, :, :, 1]], axis=-1)
        w_all = w_all.reshape(window, half)
        w = lambda i, j: w_all[i * width : (i + 1) * width, (j - 1) * width : j * width]
        f = lambda i, j: w(i, j).astype(F32)
        u = {(0, 1): -f(0, 1), (1, 2): -f(1, 2), (2, 3): -f(2, 3)}
        u[0, 2] = mm(w(0, 1), w(1, 2), None) - f(0, 2)
        u[1, 3] = mm(w(1, 2), w(2, 3), None) - f(1, 3)
        u[0, 3] = mm(w(0, 1), w(1, 3), None) - f(0, 3) - mm(u[0, 2], f(2, 3))
        columns = [
            jnp.concatenate([u[i, j] for i in range(j)], axis=0) for j in range(1, supernodes)
        ]

    def times_u(v):
        parts = [v[:, :width]]
        for j in range(1, supernodes):
            parts.append(v[:, j * width : (j + 1) * width] + mm(v[:, : j * width], columns[j - 1]))
        return jnp.concatenate(parts, axis=1)

    with jax.named_scope("cross"):
        right = times_u(product)
        left = times_u(panel_c.astype(F32))
        cross = lax.psum_scatter(
            right.reshape(ny, local, window), "y", scatter_dimension=0, tiled=True
        ).reshape(local, window)
        scale = jnp.repeat(select, width)[None, :]
        cross = -(scale * cross)

    with jax.named_scope("window"):
        tiles = []
        for t in range(supernodes):
            n = window - t * width
            part = mm_t(left[:, t * width : (t + 1) * width], right[:, t * width :])
            part = part.reshape(2, nx, nc, wlocal, n).transpose(2, 1, 3, 0, 4)
            tiles += [part[:, :, :, 0], part[:, :, :, 1]]
        packed = jnp.concatenate(tiles, axis=-1)
        packed = exchange(packed, "c").reshape(nc, nx, wlocal, -1).sum(0)
        packed = exchange(packed, "x").reshape(nx, wlocal, -1).sum(0)
        spread, at = [], 0
        for t in range(supernodes):
            n = window - t * width
            for _ in range(2):
                spread.append(jnp.pad(packed[:, at : at + n], ((0, 0), (window - n, 0))))
                at += n
        mine_w = exchange(jnp.stack(spread), "z").sum(0)
        mine_w = gather(mine_w, "y", ny).sum(0)

    with jax.named_scope("diagonal"):
        v_rows = []
        for k in range(supernodes):
            t_k = tile_inverse[k]
            blocks = [jnp.zeros((width, k * width), F32)] if k else []
            blocks.append(t_k)
            if k + 1 < supernodes:
                u_row = jnp.concatenate([u[k, j] for j in range(k + 1, supernodes)], axis=1)
                blocks.append(mm(t_k, u_row))
            v_rows.append(jnp.concatenate(blocks, axis=1))
        v_all = jnp.concatenate(v_rows, axis=0)
        v_mine = lax.dynamic_slice_in_dim(v_all, col * wlocal, wlocal, 1)
        base = mm_t(v_mine, v_all)
        keep = (jnp.arange(window, dtype=jnp.int32) // width) >= wtile
        block = jnp.where(keep[None, :], mine_w + base, 0.0)
    return cross, block


def solution(mesh):
    fine = Mesh(mesh.devices.reshape(8, 8, 4, 2), ("y", "z", "x", "c"))
    col = ("z", "x", "c")
    return jax.shard_map(
        body,
        mesh=fine,
        in_specs=(P("y", None, col, None), P(("y",) + col, None), P(col, None), P(), P()),
        out_specs=(P(("y",) + col, None), P(col, None)),
        check_vma=False,
    )
```

```python
import jax
import jax.numpy as jnp
from jax import lax
from jax.experimental import pallas as pl
from jax.experimental.pallas import tpu as pltpu
from jax.sharding import Mesh, PartitionSpec as P

HIGHEST = lax.Precision.HIGHEST
HIGH = lax.Precision.HIGH
BF16 = jnp.bfloat16
F32 = jnp.float32


def mm(a, b, precision=HIGH):
    return jnp.dot(a, b, precision=precision, preferred_element_type=F32)


def mm_t(a, b, precision=HIGH):
    return lax.dot_general(
        a, b, (((0,), (0,)), ((), ())), precision=precision, preferred_element_type=F32
    )


def exchange(x, axis):
    return lax.all_to_all(x, axis, 0, 0, tiled=True)


def gather(x, axis, size):
    return exchange(jnp.broadcast_to(x[None], (size,) + x.shape), axis)


def local_call(kernel, shapes, scalars, *arrays):
    vmem = pl.BlockSpec(memory_space=pltpu.VMEM)
    smem = pl.BlockSpec(memory_space=pltpu.SMEM)
    return pl.pallas_call(
        kernel,
        out_shape=shapes,
        in_specs=[smem] * len(scalars) + [vmem] * len(arrays),
        out_specs=jax.tree.map(lambda _: vmem, shapes),
        compiler_params=pltpu.CompilerParams(vmem_limit_bytes=40 * 1024 * 1024),
    )(*scalars, *arrays)


def panel_kernel(scale_ref, a_ref, w_ref, t_ref, message_ref, panel_ref):
    supernodes, width = t_ref.shape[0], t_ref.shape[1]
    local, wlocal = a_ref.shape[0], w_ref.shape[0]
    ha = supernodes * width // 2
    hw = (supernodes - 1) * width // 2
    for h in range(2):
        message_ref[h, local:, hw:] = jnp.zeros((wlocal, ha - hw), BF16)
    for j in range(supernodes):
        at = slice(j * width, (j + 1) * width)
        rows = jnp.concatenate([a_ref[:, at], w_ref[:, at]], axis=0)
        product = mm(rows, t_ref[j], HIGHEST)
        a = (scale_ref[j] * product[:local]).astype(BF16)
        panel_ref[:, at] = a
        h, off = divmod(j * width, ha)
        message_ref[h, :local, off : off + width] = a
        if j == 0:
            continue
        w = (scale_ref[supernodes + j] * product[local:]).astype(BF16)
        for piece in range(2):
            start = (j - 1) * width + piece * (width // 2)
            h, off = divmod(start, hw)
            message_ref[h, local:, off : off + width // 2] = w[
                :, piece * (width // 2) : (piece + 1) * (width // 2)
            ]


def sum_kernel(in_ref, out_ref):
    total = in_ref[0]
    for i in range(1, in_ref.shape[0]):
        total = total + in_ref[i]
    out_ref[...] = total


def spread_kernel(in_ref, out_ref):
    width = out_ref.shape[2] // 4
    at = 0
    for i in range(out_ref.shape[0]):
        edge = (i // 2) * width
        n = out_ref.shape[2] - edge
        total = in_ref[0, :, at : at + n]
        for k in range(1, in_ref.shape[0]):
            total = total + in_ref[k, :, at : at + n]
        if edge:
            out_ref[i, :, :edge] = jnp.zeros((out_ref.shape[1], edge), F32)
        out_ref[i, :, edge:] = total
        at += n


def repeat_kernel(in_ref, out_ref):
    total = in_ref[0]
    for i in range(1, in_ref.shape[0]):
        total = total + in_ref[i]
    for i in range(out_ref.shape[0]):
        out_ref[i] = total


def finish_kernel(tile_ref, in_ref, base_ref, out_ref):
    total = base_ref[...]
    for i in range(in_ref.shape[0]):
        total = total + in_ref[i]
    columns = lax.broadcasted_iota(jnp.int32, total.shape, 1)
    out_ref[...] = jnp.where(columns >= tile_ref[0] * (total.shape[1] // 4), total, 0.0)


def body(sigma_top, ancestor_rows, window_rows, tile_inverse, structure):
    ny, nz, nx, nc = 8, 8, 4, 2
    supernodes, width = tile_inverse.shape[0], tile_inverse.shape[1]
    window = supernodes * width
    local = ancestor_rows.shape[0]
    wlocal = window_rows.shape[0]
    y, z, x, c = (lax.axis_index(name) for name in ("y", "z", "x", "c"))
    col = (z * nx + x) * nc + c
    tile = ((y * (nz * nx * nc) + col) * local) // width
    wtile = (col * wlocal) // width
    select = lax.dynamic_slice_in_dim(structure, tile, 1, 1)[:, 0].astype(F32)

    with jax.named_scope("panels"):
        ha, hw = window // 2, (window - width) // 2
        keep = (wtile < jnp.arange(supernodes, dtype=jnp.int32)).astype(F32)
        message, panel = local_call(
            panel_kernel,
            (
                jax.ShapeDtypeStruct((nc, local + wlocal, ha), BF16),
                jax.ShapeDtypeStruct((local, window), BF16),
            ),
            (jnp.concatenate([select, keep]),),
            ancestor_rows,
            window_rows,
            tile_inverse,
        )

    with jax.named_scope("gather"):
        got = exchange(message, "c").reshape(nc, local + wlocal, ha)
        got = lax.all_gather(got, "x", axis=0, tiled=True)
        half = lax.all_gather(got[:, :local].reshape(-1, ha), "z", axis=0, tiled=True)
        wgot = got[:, local:, :hw].reshape(-1, hw)
        whalf = gather(wgot, "z", nz).reshape(window, hw)[: window - width]
        swap = [(0, 1), (1, 0)]
        sibling = lax.ppermute(half, "c", swap)
        wsibling = lax.ppermute(whalf, "c", swap)
        first = c == 0

    with jax.named_scope("column_block"):
        panel_c = gather(panel, "y", ny).reshape(ny * local, window)

    with jax.named_scope("sigma"):
        sigma = sigma_top.transpose(1, 2, 3, 0).reshape(ny * local, -1)
        own = mm(sigma, half, None)
        away = mm(sigma, sibling, None)
        product = jnp.concatenate(
            [jnp.where(first, own, away), jnp.where(first, away, own)], axis=1
        )

    with jax.named_scope("unit_inverse"):
        w_all = jnp.concatenate(
            [jnp.where(first, whalf, wsibling), jnp.where(first, wsibling, whalf)], axis=1
        )
        w = lambda i, j: w_all[i * width : (i + 1) * width, (j - 1) * width : j * width]
        f = lambda i, j: w(i, j).astype(F32)
        u = {(0, 1): -f(0, 1), (1, 2): -f(1, 2), (2, 3): -f(2, 3)}
        u[0, 2] = mm(w(0, 1), w(1, 2), None) - f(0, 2)
        u[1, 3] = mm(w(1, 2), w(2, 3), None) - f(1, 3)
        u[0, 3] = mm(w(0, 1), w(1, 3), None) - f(0, 3) - mm(u[0, 2], f(2, 3))
        columns = [
            jnp.concatenate([u[i, j] for i in range(j)], axis=0) for j in range(1, supernodes)
        ]

    def times_u(v):
        parts = [v[:, :width]]
        for j in range(1, supernodes):
            parts.append(v[:, j * width : (j + 1) * width] + mm(v[:, : j * width], columns[j - 1]))
        return jnp.concatenate(parts, axis=1)

    with jax.named_scope("cross"):
        right = times_u(product)
        left = times_u(panel_c.astype(F32))
        cross = lax.psum_scatter(
            right.reshape(ny, local, window), "y", scatter_dimension=0, tiled=True
        ).reshape(local, window)
        scale = jnp.repeat(select, width)[None, :]
        cross = -(scale * cross)

    with jax.named_scope("window"):
        tiles = []
        for t in range(supernodes):
            n = window - t * width
            part = mm_t(left[:, t * width : (t + 1) * width], right[:, t * width :])
            part = part.reshape(2, nx, nc, wlocal, n).transpose(2, 1, 3, 0, 4)
            tiles += [part[:, :, :, 0], part[:, :, :, 1]]
        packed = jnp.concatenate(tiles, axis=-1)
        shape = lambda *dims: jax.ShapeDtypeStruct(dims, F32)
        n = packed.shape[-1]
        packed = exchange(packed, "c")
        packed = local_call(sum_kernel, shape(nx, wlocal, n), (), packed)
        packed = exchange(packed, "x")
        spread = local_call(spread_kernel, shape(nz, wlocal, window), (), packed)
        spread = exchange(spread, "z")
        spread = local_call(repeat_kernel, shape(ny, wlocal, window), (), spread)
        spread = exchange(spread, "y")

    with jax.named_scope("diagonal"):
        v_rows = []
        for k in range(supernodes):
            t_k = tile_inverse[k]
            blocks = [jnp.zeros((width, k * width), F32)] if k else []
            blocks.append(t_k)
            if k + 1 < supernodes:
                u_row = jnp.concatenate([u[k, j] for j in range(k + 1, supernodes)], axis=1)
                blocks.append(mm(t_k, u_row))
            v_rows.append(jnp.concatenate(blocks, axis=1))
        v_all = jnp.concatenate(v_rows, axis=0)
        v_mine = lax.dynamic_slice_in_dim(v_all, col * wlocal, wlocal, 1)
        base = mm_t(v_mine, v_all)
        block = local_call(
            finish_kernel, shape(wlocal, window), (wtile.reshape(1),), spread, base
        )
    return cross, block


def solution(mesh):
    fine = Mesh(mesh.devices.reshape(8, 8, 4, 2), ("y", "z", "x", "c"))
    col = ("z", "x", "c")
    return jax.shard_map(
        body,
        mesh=fine,
        in_specs=(P("y", None, col, None), P(("y",) + col, None), P(col, None), P(), P()),
        out_specs=(P(("y",) + col, None), P(col, None)),
        check_vma=False,
    )
```

```python
import jax
import jax.numpy as jnp
from jax import lax
from jax.experimental import pallas as pl
from jax.experimental.pallas import tpu as pltpu
from jax.sharding import Mesh, PartitionSpec as P

HIGHEST = lax.Precision.HIGHEST
HIGH = lax.Precision.HIGH
BF16 = jnp.bfloat16
F32 = jnp.float32


def mm(a, b, precision=HIGH):
    return jnp.dot(a, b, precision=precision, preferred_element_type=F32)


def exchange(x, axis):
    return lax.all_to_all(x, axis, 0, 0, tiled=True)


def gather(x, axis, size):
    return exchange(jnp.broadcast_to(x[None], (size,) + x.shape), axis)


def local_call(kernel, shapes, scalars, *arrays, scratch=()):
    vmem = pl.BlockSpec(memory_space=pltpu.VMEM)
    smem = pl.BlockSpec(memory_space=pltpu.SMEM)
    return pl.pallas_call(
        kernel,
        out_shape=shapes,
        in_specs=[smem] * len(scalars) + [vmem] * len(arrays),
        out_specs=jax.tree.map(lambda _: vmem, shapes),
        scratch_shapes=[pltpu.VMEM(*each) for each in scratch],
        compiler_params=pltpu.CompilerParams(vmem_limit_bytes=24 * 1024 * 1024),
    )(*scalars, *arrays)


def panel_kernel(structure_ref, place_ref, a_ref, w_ref, t_ref, message_ref, panel_ref):
    supernodes, width = t_ref.shape[0], t_ref.shape[1]
    local, wlocal = a_ref.shape[0], w_ref.shape[0]
    ha = supernodes * width // 2
    hw = (supernodes - 1) * width // 2
    for h in range(2):
        message_ref[h, local:, hw:] = jnp.zeros((wlocal, ha - hw), BF16)
    for j in range(supernodes):
        at = slice(j * width, (j + 1) * width)
        rows = jnp.concatenate([a_ref[:, at], w_ref[:, at]], axis=0)
        product = mm(rows, t_ref[j], HIGHEST)
        scale = structure_ref[j, place_ref[0]].astype(F32)
        a = (scale * product[:local]).astype(BF16)
        for copy in range(2):
            start = (copy * supernodes + j) * width
            panel_ref[:, start : start + width] = a
        h, off = divmod(j * width, ha)
        message_ref[h, :local, off : off + width] = a
        if j == 0:
            continue
        scale = jnp.where(place_ref[1] < j, 1.0, 0.0)
        w = (scale * product[local:]).astype(BF16)
        for half in range(2):
            message_ref[half, local:, (j - 1) * width // 2 : j * width // 2] = w[
                :, half * width // 2 : (half + 1) * width // 2
            ]


def pack_kernel(got_ref, out_ref):
    blocks, height, columns = got_ref.shape
    rows = (out_ref.shape[0] - 96) // blocks
    edge = rows * blocks
    half = columns // 4
    for i in range(blocks):
        out_ref[i * rows : (i + 1) * rows] = got_ref[i, :rows]
    for k in range(2):
        for c in range(2):
            at = edge + (2 * k + c) * 16
            block = 2 * k + c
            out_ref[at : at + 16, : 3 * half] = got_ref[block, rows:, : 3 * half]
            out_ref[at : at + 16, 3 * half :] = got_ref[8 + block, rows:, 2 * half : 3 * half]
            at = edge + 64 + c * 16
            out_ref[at : at + 16, 2 * k * half : 2 * (k + 1) * half] = got_ref[
                4 + block, rows:, half : 3 * half
            ]


def split(v):
    high = v.astype(BF16)
    return high, (v - high.astype(F32)).astype(BF16)


def dot(a, b):
    return jnp.dot(a, b, preferred_element_type=F32)


def dot_t(a, b):
    return lax.dot_general(a, b, (((0,), (0,)), ((), ())), preferred_element_type=F32)


def product_kernel(x_ref, sigma_ref, p0_ref, p1_ref, p2_ref, p3_ref, out_ref, held_ref):
    nz, nx, rows, columns = held_ref.shape
    for shift, ref in enumerate((p0_ref, p1_ref, p2_ref, p3_ref)):
        source = lax.rem(x_ref[0] + nx - shift, nx)
        for i in range(nz):
            held_ref[i, source] = ref[i * rows : (i + 1) * rows]
    out_ref[...] = dot(sigma_ref[...], held_ref[...].reshape(nz * nx * rows, columns))


def inverse_kernel(core_ref, x_ref, *refs):
    pieces, (high_ref, low_ref, held_ref) = refs[:8], refs[8:]
    width = high_ref.shape[0] // 3
    half = width // 2
    nx = held_ref.shape[3]
    edge = pieces[0].shape[0] - 96
    for group in range(2):
        side = core_ref[0] if group == 0 else 1 - core_ref[0]
        for shift in range(nx):
            ref = pieces[group * nx + shift]
            source = lax.rem(x_ref[0] + nx - shift, nx)
            for k in range(2):
                at = slice(edge + k * 32, edge + (k + 1) * 32)
                held_ref[side, 0, k, source] = ref[at, : 3 * half]
                held_ref[side, 1, k, source, :, half:] = ref[
                    edge + 64 : edge + 96, 2 * k * half : 2 * (k + 1) * half
                ]
                held_ref[side, 2, k, source, :, 2 * half :] = ref[at, 3 * half :]
    w = lambda i, j: jnp.concatenate(
        [
            held_ref[side, i, :, :, :, (j - 1) * half : j * half].reshape(width, half)
            for side in range(2)
        ],
        axis=1,
    )
    f = lambda i, j: w(i, j).astype(F32)
    u = {(i, i + 1): -f(i, i + 1) for i in range(3)}
    u[0, 2] = dot(w(0, 1), w(1, 2)) - f(0, 2)
    u[1, 3] = dot(w(1, 2), w(2, 3)) - f(1, 3)
    high, low = split(u[0, 2])
    u[0, 3] = dot(w(0, 1), w(1, 3)) - f(0, 3) - dot(high, w(2, 3)) - dot(low, w(2, 3))
    for i in range(3):
        for j in range(1, 4):
            at = (slice(i * width, (i + 1) * width), slice((j - 1) * width, j * width))
            value = u.get((i, j))
            value = jnp.zeros((width, width), F32) if value is None else value
            high_ref[at], low_ref[at] = split(value)


def left_kernel(panel_ref, high_ref, low_ref, lh_ref, ll_ref):
    width = lh_ref.shape[1] // 4
    lh_ref[:, :width] = panel_ref[:, :width]
    ll_ref[:, :width] = jnp.zeros((panel_ref.shape[0], width), BF16)
    for j in range(1, 4):
        a = panel_ref[:, : j * width]
        at = (slice(0, j * width), slice((j - 1) * width, j * width))
        value = panel_ref[:, j * width : (j + 1) * width].astype(F32)
        value = value + dot(a, high_ref[at]) + dot(a, low_ref[at])
        cut = slice(j * width, (j + 1) * width)
        lh_ref[:, cut], ll_ref[:, cut] = split(value)


def window_kernel(
    core_ref, mine_ref, other_ref, high_ref, low_ref, lh_ref, ll_ref,
    right_ref, keep_ref, send_ref, packed_ref, rh_ref, rl_ref, fh_ref, fl_ref,
):
    nc, nx, rows, _ = packed_ref.shape
    size, window = rh_ref.shape
    width = window // 4
    first = core_ref[0] == 0
    ny, local = right_ref.shape[0], right_ref.shape[1]
    fs = []
    for h in range(2):
        a, b = (mine_ref, other_ref) if h == 0 else (other_ref, mine_ref)
        value = jnp.where(first, a[...], b[...])
        at = slice(h * window // 2, (h + 1) * window // 2)
        fh_ref[:, at], fl_ref[:, at] = split(value)
        fs += [value[:, :width], value[:, width:]]
    for j in range(4):
        value = fs[j]
        if j:
            at = (slice(0, j * width), slice((j - 1) * width, j * width))
            fh = fh_ref[:, : j * width]
            value = value + (
                dot(fh, high_ref[at]) + dot(fl_ref[:, : j * width], high_ref[at]) + dot(fh, low_ref[at])
            )
        cut = slice(j * width, (j + 1) * width)
        for i in range(ny):
            right_ref[i, :, cut] = value[i * local : (i + 1) * local]
        rh_ref[:, cut], rl_ref[:, cut] = split(value)
    at = 0
    for t in range(4):
        n = window - t * width
        cut = slice(t * width, (t + 1) * width)
        lh, ll = lh_ref[:, cut], ll_ref[:, cut]
        rh, rl = rh_ref[:, t * width :], rl_ref[:, t * width :]
        part = dot_t(lh, rh) + dot_t(ll, rh) + dot_t(lh, rl)
        for k in range(2):
            for i in range(nx):
                for c in range(nc):
                    row = ((k * nx + i) * nc + c) * rows
                    packed_ref[c, i, :, at : at + n] = part[row : row + rows]
            at += n
    keep_ref[...] = packed_ref[core_ref[0]]
    send_ref[...] = packed_ref[1 - core_ref[0]]


def exponent(v):
    top = jnp.max(jnp.abs(v), axis=(0, 1), keepdims=True)
    return jnp.floor(jnp.log2(jnp.maximum(top, 1e-30))) - 13.0


def sum_kernel(a_ref, b_ref, out_ref):
    nx, rows, n = a_ref.shape
    for i in range(nx):
        total = a_ref[i] + b_ref[i]
        power = exponent(total)
        out_ref[i, :, :n] = total * jnp.exp2(-power)
        out_ref[i, :, n:] = jnp.broadcast_to(power, (rows, out_ref.shape[2] - n))


def spread_kernel(in_ref, out_ref):
    size, rows, window = out_ref.shape[0], out_ref.shape[1], out_ref.shape[2] - 128
    width = window // 4
    last = in_ref.shape[2] - 128
    scales = [jnp.exp2(in_ref[k, :, last : last + 1]) for k in range(in_ref.shape[0])]
    at = 0
    for i in range(size):
        edge = (i // 2) * width
        n = window - edge
        total = in_ref[0, :, at : at + n] * scales[0]
        for k in range(1, in_ref.shape[0]):
            total = total + in_ref[k, :, at : at + n] * scales[k]
        power = exponent(total)
        if edge:
            out_ref[i, :, :edge] = jnp.zeros((rows, edge), F32)
        out_ref[i, :, edge:window] = total * jnp.exp2(-power)
        out_ref[i, :, window:] = jnp.broadcast_to(power, (rows, 128))
        at += n


def repeat_kernel(in_ref, out_ref):
    window = out_ref.shape[1] - 128
    total = jnp.zeros((out_ref.shape[0], window), F32)
    for i in range(in_ref.shape[0]):
        total = total + in_ref[i, :, :window] * jnp.exp2(in_ref[i, :, window : window + 1])
    power = exponent(total)
    out_ref[:, :window] = total * jnp.exp2(-power)
    out_ref[:, window:] = jnp.broadcast_to(power, (out_ref.shape[0], 128))


def finish_kernel(tile_ref, in_ref, base_ref, out_ref):
    total = base_ref[...]
    window = total.shape[1]
    for i in range(in_ref.shape[0]):
        total = total + in_ref[i, :, :window] * jnp.exp2(in_ref[i, :, window : window + 1])
    columns = lax.broadcasted_iota(jnp.int32, total.shape, 1)
    out_ref[...] = jnp.where(columns >= tile_ref[0] * (window // 4), total, 0.0)


def base_kernel(place_ref, t_ref, high_ref, low_ref, out_ref, vh_ref, vl_ref, rows_ref):
    n, width = t_ref.shape[0], t_ref.shape[1]
    for k in range(n):
        th, tl = split(t_ref[k])
        down = slice(k * width, (k + 1) * width)
        for j in range(n):
            if j < k:
                zero = jnp.zeros((width, width), BF16)
                vh_ref[j, down], vl_ref[j, down] = zero, zero
            elif j == k:
                vh_ref[j, down], vl_ref[j, down] = th, tl
            else:
                at = (down, slice((j - 1) * width, j * width))
                value = dot(th, high_ref[at]) + dot(tl, high_ref[at]) + dot(th, low_ref[at])
                vh_ref[j, down], vl_ref[j, down] = split(value)
    ah, al = vh_ref[place_ref[1]], vl_ref[place_ref[1]]
    for j in range(n):
        vh, vl = vh_ref[j], vl_ref[j]
        rows_ref[:, j * width : (j + 1) * width] = dot_t(ah, vh) + dot_t(al, vh) + dot_t(ah, vl)
    rows = out_ref.shape[0]
    out_ref[...] = rows_ref[pl.ds(pl.multiple_of(place_ref[2] * rows, rows), rows)]


def body(sigma_top, ancestor_rows, window_rows, tile_inverse, structure):
    ny, nz, nx, nc = 8, 8, 4, 2
    supernodes, width = tile_inverse.shape[0], tile_inverse.shape[1]
    window = supernodes * width
    local = ancestor_rows.shape[0]
    wlocal = window_rows.shape[0]
    y, z, x, c = (lax.axis_index(name) for name in ("y", "z", "x", "c"))
    col = (z * nx + x) * nc + c
    tile = ((y * (nz * nx * nc) + col) * local) // width
    wtile = (col * wlocal) // width
    select = lax.dynamic_slice_in_dim(structure, tile, 1, 1)[:, 0].astype(F32)

    with jax.named_scope("panels"):
        ha, hw = window // 2, (window - width) // 2
        place = jnp.stack([tile, wtile, col % (width // wlocal)])
        message, panel = local_call(
            panel_kernel,
            (
                jax.ShapeDtypeStruct((nc, local + wlocal, ha), BF16),
                jax.ShapeDtypeStruct((local, 2 * window), BF16),
            ),
            (structure, place),
            ancestor_rows,
            window_rows,
            tile_inverse,
        )

    shape = lambda *dims, dtype=F32: jax.ShapeDtypeStruct(dims, dtype)
    with jax.named_scope("column_block"):
        panel_c = lax.all_gather(panel, "y", axis=0, tiled=True)

    with jax.named_scope("gather"):
        got = exchange(message, "c").reshape(nc, local + wlocal, ha)
        got = lax.all_gather(got, "z", axis=0, tiled=True)
        swap = [(0, 1), (1, 0)]
        first = local_call(
            pack_kernel, shape(nz * nc * local + 96, ha, dtype=BF16), (), got
        )
        pieces = [first]
        for step in range(1, nx):
            pieces.append(
                lax.ppermute(first, "x", [(i, (i + step) % nx) for i in range(nx)])
            )
        others = [lax.ppermute(piece, "c", swap) for piece in pieces]

    with jax.named_scope("unit_inverse"):
        core = c.reshape(1)
        n = window - width
        high, low = local_call(
            inverse_kernel,
            (shape(n, n, dtype=BF16), shape(n, n, dtype=BF16)),
            (core, x.reshape(1)),
            *pieces,
            *others,
            scratch=(((2, supernodes - 1, 2, nx, 2 * wlocal, n // 2), BF16),),
        )
        lh, ll = local_call(
            left_kernel,
            (shape(ny * local, window, dtype=BF16),) * 2,
            (),
            panel_c,
            high,
            low,
        )

    with jax.named_scope("product"):
        sigma = sigma_top.transpose(1, 2, 3, 0).reshape(ny * local, -1)
        held = (((nz, nx, nc * local, ha), BF16),)
        product = lambda parts: local_call(
            product_kernel,
            shape(ny * local, ha),
            (x.reshape(1),),
            sigma,
            *parts,
            scratch=held,
        )
        own = product(pieces)
        away = product(others)

    with jax.named_scope("window"):
        half = ((ny * local, window), BF16)
        packed = (nx, wlocal, 2 * 10 * width)
        right, keep, send = local_call(
            window_kernel,
            (shape(ny, local, window), shape(*packed), shape(*packed)),
            (core,),
            own,
            away,
            high,
            low,
            lh,
            ll,
            scratch=(((nc,) + packed, F32), half, half, half, half),
        )
        cross = lax.psum_scatter(right, "y", scatter_dimension=0, tiled=True)
        scale = jnp.repeat(select, width)[None, :]
        cross = -(scale * cross.reshape(local, window))
        came = lax.ppermute(send, "c", swap)
        half_type = jnp.float16
        n = packed[-1] + 128
        parts = local_call(sum_kernel, shape(nx, wlocal, n), (), keep, came)
        parts = exchange(parts.astype(half_type), "x").astype(F32)
        spread = local_call(spread_kernel, shape(nz, wlocal, window + 128), (), parts)
        spread = exchange(spread.astype(half_type), "z").astype(F32)
        spread = local_call(repeat_kernel, shape(wlocal, window + 128), (), spread)
        spread = gather(spread.astype(half_type), "y", ny).astype(F32)

    with jax.named_scope("diagonal"):
        spare = ((supernodes, window, width), BF16)
        base = local_call(
            base_kernel,
            shape(wlocal, window),
            (place,),
            tile_inverse,
            high,
            low,
            scratch=(spare, spare, ((width, window), F32)),
        )
        block = local_call(
            finish_kernel, shape(wlocal, window), (wtile.reshape(1),), spread, base
        )
    return cross, block


def solution(mesh):
    fine = Mesh(mesh.devices.reshape(8, 8, 4, 2), ("y", "z", "x", "c"))
    col = ("z", "x", "c")
    return jax.shard_map(
        body,
        mesh=fine,
        in_specs=(P("y", None, col, None), P(("y",) + col, None), P(col, None), P(), P()),
        out_specs=(P(("y",) + col, None), P(col, None)),
        check_vma=False,
    )
```

```python
import jax
import jax.numpy as jnp
from jax import lax
from jax.experimental import pallas as pl
from jax.experimental.pallas import tpu as pltpu
from jax.sharding import Mesh, PartitionSpec as P

HIGHEST = lax.Precision.HIGHEST
HIGH = lax.Precision.HIGH
BF16 = jnp.bfloat16
F32 = jnp.float32


def mm(a, b, precision=HIGH):
    return jnp.dot(a, b, precision=precision, preferred_element_type=F32)


def exchange(x, axis):
    return lax.all_to_all(x, axis, 0, 0, tiled=True)


def gather(x, axis, size):
    return exchange(jnp.broadcast_to(x[None], (size,) + x.shape), axis)


def local_call(kernel, shapes, scalars, *arrays, scratch=(), far=False, mebibytes=24):
    vmem = pl.BlockSpec(memory_space=pltpu.VMEM)
    smem = pl.BlockSpec(memory_space=pltpu.SMEM)
    array_spec = pl.BlockSpec(memory_space=pl.ANY) if far else vmem
    return pl.pallas_call(
        kernel,
        out_shape=shapes,
        in_specs=[smem] * len(scalars) + [array_spec] * len(arrays),
        out_specs=jax.tree.map(lambda _: vmem, shapes),
        scratch_shapes=[
            pltpu.VMEM(*each) if isinstance(each, tuple) else each for each in scratch
        ],
        compiler_params=pltpu.CompilerParams(vmem_limit_bytes=mebibytes * 1024 * 1024),
    )(*scalars, *arrays)


def panel_kernel(
    place_ref, structure_far, a_far, w_far, t_far, message_ref, panel_ref,
    structure_ref, a_ref, w_ref, t_ref, sems,
):
    pairs = [(structure_far, structure_ref), (a_far, a_ref), (w_far, w_ref)]
    pairs += [(t_far.at[j], t_ref.at[j]) for j in range(t_ref.shape[0])]
    copies = [
        pltpu.make_async_copy(here, there, sems.at[i]) for i, (here, there) in enumerate(pairs)
    ]
    for copy in copies:
        copy.start()
    for copy in copies[:3]:
        copy.wait()
    supernodes, width = t_ref.shape[0], t_ref.shape[1]
    local, wlocal = a_ref.shape[0], w_ref.shape[0]
    ha = supernodes * width // 2
    hw = (supernodes - 1) * width // 2
    for h in range(2):
        message_ref[h, local:, hw:] = jnp.zeros((wlocal, ha - hw), BF16)
    for j in range(supernodes):
        at = slice(j * width, (j + 1) * width)
        rows = jnp.concatenate([a_ref[:, at], w_ref[:, at]], axis=0)
        copies[3 + j].wait()
        product = mm(rows, t_ref[j], HIGHEST)
        scale = structure_ref[j, place_ref[0]].astype(F32)
        a = (scale * product[:local]).astype(BF16)
        for copy in range(2):
            start = (copy * supernodes + j) * width
            panel_ref[:, start : start + width] = a
        h, off = divmod(j * width, ha)
        message_ref[h, :local, off : off + width] = a
        if j == 0:
            continue
        scale = jnp.where(place_ref[1] < j, 1.0, 0.0)
        w = (scale * product[local:]).astype(BF16)
        for half in range(2):
            message_ref[half, local:, (j - 1) * width // 2 : j * width // 2] = w[
                :, half * width // 2 : (half + 1) * width // 2
            ]


def pack_kernel(got_ref, out_ref):
    blocks, height, columns = got_ref.shape
    rows = (out_ref.shape[0] - 96) // blocks
    edge = rows * blocks
    half = columns // 4
    for i in range(blocks):
        out_ref[i * rows : (i + 1) * rows] = got_ref[i, :rows]
    for k in range(2):
        for c in range(2):
            at = edge + (2 * k + c) * 16
            block = 2 * k + c
            out_ref[at : at + 16, : 3 * half] = got_ref[block, rows:, : 3 * half]
            out_ref[at : at + 16, 3 * half :] = got_ref[8 + block, rows:, 2 * half : 3 * half]
            at = edge + 64 + c * 16
            out_ref[at : at + 16, 2 * k * half : 2 * (k + 1) * half] = got_ref[
                4 + block, rows:, half : 3 * half
            ]


def split(v):
    high = v.astype(BF16)
    return high, (v - high.astype(F32)).astype(BF16)


def dot(a, b):
    return jnp.dot(a, b, preferred_element_type=F32)


def dot_t(a, b):
    return lax.dot_general(a, b, (((0,), (0,)), ((), ())), preferred_element_type=F32)


def product_kernel(x_ref, sigma_ref, p0_ref, p1_ref, p2_ref, p3_ref, out_ref, held_ref):
    nz, nx, rows, columns = held_ref.shape
    for shift, ref in enumerate((p0_ref, p1_ref, p2_ref, p3_ref)):
        source = lax.rem(x_ref[0] + nx - shift, nx)
        for i in range(nz):
            held_ref[i, source] = ref[i * rows : (i + 1) * rows]
    out_ref[...] = dot(sigma_ref[...], held_ref[...].reshape(nz * nx * rows, columns))


def inverse_kernel(core_ref, x_ref, *refs):
    pieces, (high_ref, low_ref, held_ref) = refs[:8], refs[8:]
    width = high_ref.shape[0] // 3
    half = width // 2
    nx = held_ref.shape[3]
    edge = pieces[0].shape[0] - 96
    for group in range(2):
        side = core_ref[0] if group == 0 else 1 - core_ref[0]
        for shift in range(nx):
            ref = pieces[group * nx + shift]
            source = lax.rem(x_ref[0] + nx - shift, nx)
            for k in range(2):
                at = slice(edge + k * 32, edge + (k + 1) * 32)
                held_ref[side, 0, k, source] = ref[at, : 3 * half]
                held_ref[side, 1, k, source, :, half:] = ref[
                    edge + 64 : edge + 96, 2 * k * half : 2 * (k + 1) * half
                ]
                held_ref[side, 2, k, source, :, 2 * half :] = ref[at, 3 * half :]
    w = lambda i, j: jnp.concatenate(
        [
            held_ref[side, i, :, :, :, (j - 1) * half : j * half].reshape(width, half)
            for side in range(2)
        ],
        axis=1,
    )
    f = lambda i, j: w(i, j).astype(F32)
    u = {(i, i + 1): -f(i, i + 1) for i in range(3)}
    u[0, 2] = dot(w(0, 1), w(1, 2)) - f(0, 2)
    u[1, 3] = dot(w(1, 2), w(2, 3)) - f(1, 3)
    high, low = split(u[0, 2])
    u[0, 3] = dot(w(0, 1), w(1, 3)) - f(0, 3) - dot(high, w(2, 3)) - dot(low, w(2, 3))
    for i in range(3):
        for j in range(1, 4):
            at = (slice(i * width, (i + 1) * width), slice((j - 1) * width, j * width))
            value = u.get((i, j))
            value = jnp.zeros((width, width), F32) if value is None else value
            high_ref[at], low_ref[at] = split(value)


def left_kernel(panel_ref, high_ref, low_ref, lh_ref, ll_ref):
    width = lh_ref.shape[1] // 4
    lh_ref[:, :width] = panel_ref[:, :width]
    ll_ref[:, :width] = jnp.zeros((panel_ref.shape[0], width), BF16)
    for j in range(1, 4):
        a = panel_ref[:, : j * width]
        at = (slice(0, j * width), slice((j - 1) * width, j * width))
        value = panel_ref[:, j * width : (j + 1) * width].astype(F32)
        value = value + dot(a, high_ref[at]) + dot(a, low_ref[at])
        cut = slice(j * width, (j + 1) * width)
        lh_ref[:, cut], ll_ref[:, cut] = split(value)


def window_kernel(
    core_ref, mine_ref, other_ref, high_ref, low_ref, lh_ref, ll_ref,
    right_ref, packed_ref, rh_ref, rl_ref, fh_ref, fl_ref,
):
    nc, nx, rows, _ = packed_ref.shape
    size, window = rh_ref.shape
    width = window // 4
    first = core_ref[0] == 0
    ny, local = right_ref.shape[0], right_ref.shape[1]
    fs = []
    for h in range(2):
        a, b = (mine_ref, other_ref) if h == 0 else (other_ref, mine_ref)
        value = jnp.where(first, a[...], b[...])
        at = slice(h * window // 2, (h + 1) * window // 2)
        fh_ref[:, at], fl_ref[:, at] = split(value)
        fs += [value[:, :width], value[:, width:]]
    for j in range(4):
        value = fs[j]
        if j:
            at = (slice(0, j * width), slice((j - 1) * width, j * width))
            fh = fh_ref[:, : j * width]
            value = value + (
                dot(fh, high_ref[at]) + dot(fl_ref[:, : j * width], high_ref[at]) + dot(fh, low_ref[at])
            )
        cut = slice(j * width, (j + 1) * width)
        for i in range(ny):
            right_ref[i, :, cut] = value[i * local : (i + 1) * local]
        rh_ref[:, cut], rl_ref[:, cut] = split(value)
    at = 0
    for t in range(4):
        n = window - t * width
        cut = slice(t * width, (t + 1) * width)
        lh, ll = lh_ref[:, cut], ll_ref[:, cut]
        rh, rl = rh_ref[:, t * width :], rl_ref[:, t * width :]
        part = dot_t(lh, rh) + dot_t(ll, rh) + dot_t(lh, rl)
        for k in range(2):
            for i in range(nx):
                for c in range(nc):
                    row = ((k * nx + i) * nc + c) * rows
                    packed_ref[c, i, :, at : at + n] = part[row : row + rows]
            at += n


def exponent(v):
    top = jnp.max(jnp.abs(v), axis=(0, 1), keepdims=True)
    return jnp.floor(jnp.log2(jnp.maximum(top, 1e-30))) - 13.0


def sum_kernel(in_ref, out_ref):
    _, nx, rows, n = in_ref.shape
    for i in range(nx):
        total = in_ref[0, i] + in_ref[1, i]
        power = exponent(total)
        out_ref[i, :, :n] = total * jnp.exp2(-power)
        out_ref[i, :, n:] = jnp.broadcast_to(power, (rows, out_ref.shape[2] - n))


def spread_kernel(in_ref, out_ref):
    size, rows, window = out_ref.shape[0], out_ref.shape[1], out_ref.shape[2] - 128
    width = window // 4
    last = in_ref.shape[2] - 128
    scales = [jnp.exp2(in_ref[k, :, last : last + 1]) for k in range(in_ref.shape[0])]
    at = 0
    for i in range(size):
        edge = (i // 2) * width
        n = window - edge
        total = in_ref[0, :, at : at + n] * scales[0]
        for k in range(1, in_ref.shape[0]):
            total = total + in_ref[k, :, at : at + n] * scales[k]
        power = exponent(total)
        if edge:
            out_ref[i, :, :edge] = jnp.zeros((rows, edge), F32)
        out_ref[i, :, edge:window] = total * jnp.exp2(-power)
        out_ref[i, :, window:] = jnp.broadcast_to(power, (rows, 128))
        at += n


def repeat_kernel(in_ref, out_ref):
    window = out_ref.shape[1] - 128
    total = jnp.zeros((out_ref.shape[0], window), F32)
    for i in range(in_ref.shape[0]):
        total = total + in_ref[i, :, :window] * jnp.exp2(in_ref[i, :, window : window + 1])
    power = exponent(total)
    out_ref[:, :window] = total * jnp.exp2(-power)
    out_ref[:, window:] = jnp.broadcast_to(power, (out_ref.shape[0], 128))


def finish_kernel(tile_ref, in_ref, base_ref, out_ref):
    total = base_ref[...]
    window = total.shape[1]
    for i in range(in_ref.shape[0]):
        total = total + in_ref[i, :, :window] * jnp.exp2(in_ref[i, :, window : window + 1])
    columns = lax.broadcasted_iota(jnp.int32, total.shape, 1)
    out_ref[...] = jnp.where(columns >= tile_ref[0] * (window // 4), total, 0.0)


def base_kernel(place_ref, t_ref, high_ref, low_ref, out_ref, vh_ref, vl_ref, rows_ref):
    n, width = t_ref.shape[0], t_ref.shape[1]
    for k in range(n):
        th, tl = split(t_ref[k])
        down = slice(k * width, (k + 1) * width)
        for j in range(n):
            if j < k:
                zero = jnp.zeros((width, width), BF16)
                vh_ref[j, down], vl_ref[j, down] = zero, zero
            elif j == k:
                vh_ref[j, down], vl_ref[j, down] = th, tl
            else:
                at = (down, slice((j - 1) * width, j * width))
                value = dot(th, high_ref[at]) + dot(tl, high_ref[at]) + dot(th, low_ref[at])
                vh_ref[j, down], vl_ref[j, down] = split(value)
    ah, al = vh_ref[place_ref[1]], vl_ref[place_ref[1]]
    for j in range(n):
        vh, vl = vh_ref[j], vl_ref[j]
        rows_ref[:, j * width : (j + 1) * width] = dot_t(ah, vh) + dot_t(al, vh) + dot_t(ah, vl)
    rows = out_ref.shape[0]
    out_ref[...] = rows_ref[pl.ds(pl.multiple_of(place_ref[2] * rows, rows), rows)]


def body(sigma_top, ancestor_rows, window_rows, tile_inverse, structure):
    ny, nz, nx, nc = 8, 8, 4, 2
    supernodes, width = tile_inverse.shape[0], tile_inverse.shape[1]
    window = supernodes * width
    local = ancestor_rows.shape[0]
    wlocal = window_rows.shape[0]
    y, z, x, c = (lax.axis_index(name) for name in ("y", "z", "x", "c"))
    col = (z * nx + x) * nc + c
    tile = ((y * (nz * nx * nc) + col) * local) // width
    wtile = (col * wlocal) // width
    select = lax.dynamic_slice_in_dim(structure, tile, 1, 1)[:, 0].astype(F32)

    with jax.named_scope("panels"):
        ha, hw = window // 2, (window - width) // 2
        place = jnp.stack([tile, wtile, col % (width // wlocal)])
        message, panel = local_call(
            panel_kernel,
            (
                jax.ShapeDtypeStruct((nc, local + wlocal, ha), BF16),
                jax.ShapeDtypeStruct((local, 2 * window), BF16),
            ),
            (place,),
            structure,
            ancestor_rows,
            window_rows,
            tile_inverse,
            scratch=(
                pltpu.SMEM(structure.shape, jnp.int32),
                (ancestor_rows.shape, F32),
                (window_rows.shape, F32),
                (tile_inverse.shape, F32),
                pltpu.SemaphoreType.DMA((3 + supernodes,)),
            ),
            far=True,
            mebibytes=56,
        )

    shape = lambda *dims, dtype=F32: jax.ShapeDtypeStruct(dims, dtype)
    with jax.named_scope("column_block"):
        panel_c = lax.all_gather(panel, "y", axis=0, tiled=True)

    with jax.named_scope("gather"):
        got = exchange(message, "c").reshape(nc, local + wlocal, ha)
        got = lax.all_gather(got, "z", axis=0, tiled=True)
        swap = [(0, 1), (1, 0)]
        first = local_call(
            pack_kernel, shape(nz * nc * local + 96, ha, dtype=BF16), (), got
        )
        pieces = [first]
        for step in range(1, nx):
            pieces.append(
                lax.ppermute(first, "x", [(i, (i + step) % nx) for i in range(nx)])
            )
        others = [lax.ppermute(piece, "c", swap) for piece in pieces]

    with jax.named_scope("unit_inverse"):
        core = c.reshape(1)
        n = window - width
        high, low = local_call(
            inverse_kernel,
            (shape(n, n, dtype=BF16), shape(n, n, dtype=BF16)),
            (core, x.reshape(1)),
            *pieces,
            *others,
            scratch=(((2, supernodes - 1, 2, nx, 2 * wlocal, n // 2), BF16),),
        )
        lh, ll = local_call(
            left_kernel,
            (shape(ny * local, window, dtype=BF16),) * 2,
            (),
            panel_c,
            high,
            low,
        )

    with jax.named_scope("product"):
        sigma = sigma_top.transpose(1, 2, 3, 0).reshape(ny * local, -1)
        held = (((nz, nx, nc * local, ha), BF16),)
        product = lambda parts: local_call(
            product_kernel,
            shape(ny * local, ha),
            (x.reshape(1),),
            sigma,
            *parts,
            scratch=held,
        )
        own = product(pieces)
        away = product(others)

    with jax.named_scope("window"):
        half = ((ny * local, window), BF16)
        packed = (nx, wlocal, 2 * 10 * width)
        right, packed_sum = local_call(
            window_kernel,
            (shape(ny, local, window), shape(nc, *packed)),
            (core,),
            own,
            away,
            high,
            low,
            lh,
            ll,
            scratch=(half, half, half, half),
        )
        cross = lax.psum_scatter(right, "y", scatter_dimension=0, tiled=True)
        scale = jnp.repeat(select, width)[None, :]
        cross = -(scale * cross.reshape(local, window))
        packed_sum = exchange(packed_sum, "c").reshape(nc, *packed)
        half_type = jnp.float16
        n = packed[-1] + 128
        parts = local_call(sum_kernel, shape(nx, wlocal, n), (), packed_sum)
        parts = exchange(parts.astype(half_type), "x").astype(F32)
        spread = local_call(spread_kernel, shape(nz, wlocal, window + 128), (), parts)
        spread = exchange(spread.astype(half_type), "z").astype(F32)
        spread = local_call(repeat_kernel, shape(wlocal, window + 128), (), spread)
        spread = gather(spread.astype(half_type), "y", ny).astype(F32)

    with jax.named_scope("diagonal"):
        spare = ((supernodes, window, width), BF16)
        base = local_call(
            base_kernel,
            shape(wlocal, window),
            (place,),
            tile_inverse,
            high,
            low,
            scratch=(spare, spare, ((width, window), F32)),
        )
        base, cross = lax.optimization_barrier((base, cross))
        block = local_call(
            finish_kernel, shape(wlocal, window), (wtile.reshape(1),), spread, base
        )
    return cross, block


def solution(mesh):
    fine = Mesh(mesh.devices.reshape(8, 8, 4, 2), ("y", "z", "x", "c"))
    col = ("z", "x", "c")
    return jax.shard_map(
        body,
        mesh=fine,
        in_specs=(P("y", None, col, None), P(("y",) + col, None), P(col, None), P(), P()),
        out_specs=(P(("y",) + col, None), P(col, None)),
        check_vma=False,
    )
```

```python
import jax
import jax.numpy as jnp
from jax import lax
from jax.experimental import pallas as pl
from jax.experimental.pallas import tpu as pltpu
from jax.sharding import Mesh, PartitionSpec as P

HIGHEST = lax.Precision.HIGHEST
HIGH = lax.Precision.HIGH
BF16 = jnp.bfloat16
F32 = jnp.float32


def mm(a, b, precision=HIGH):
    return jnp.dot(a, b, precision=precision, preferred_element_type=F32)


def exchange(x, axis):
    return lax.all_to_all(x, axis, 0, 0, tiled=True)


def gather(x, axis, size):
    return exchange(jnp.broadcast_to(x[None], (size,) + x.shape), axis)


def local_call(kernel, shapes, scalars, *arrays, scratch=(), far=False, mebibytes=24):
    vmem = pl.BlockSpec(memory_space=pltpu.VMEM)
    smem = pl.BlockSpec(memory_space=pltpu.SMEM)
    array_spec = pl.BlockSpec(memory_space=pl.ANY) if far else vmem
    return pl.pallas_call(
        kernel,
        out_shape=shapes,
        in_specs=[smem] * len(scalars) + [array_spec] * len(arrays),
        out_specs=jax.tree.map(lambda _: vmem, shapes),
        scratch_shapes=[
            pltpu.VMEM(*each) if isinstance(each, tuple) else each for each in scratch
        ],
        compiler_params=pltpu.CompilerParams(vmem_limit_bytes=mebibytes * 1024 * 1024),
    )(*scalars, *arrays)


def panel_kernel(
    place_ref, structure_far, a_far, w_far, t_far, message_ref, panel_ref,
    structure_ref, a_ref, w_ref, t_ref, sems,
):
    pairs = [(structure_far, structure_ref), (a_far, a_ref), (w_far, w_ref)]
    pairs += [(t_far.at[j], t_ref.at[j]) for j in range(t_ref.shape[0])]
    copies = [
        pltpu.make_async_copy(here, there, sems.at[i]) for i, (here, there) in enumerate(pairs)
    ]
    for copy in copies:
        copy.start()
    for copy in copies[:3]:
        copy.wait()
    supernodes, width = t_ref.shape[0], t_ref.shape[1]
    local, wlocal = a_ref.shape[0], w_ref.shape[0]
    ha = supernodes * width // 2
    hw = (supernodes - 1) * width // 2
    for h in range(2):
        message_ref[h, local:, hw:] = jnp.zeros((wlocal, ha - hw), BF16)
    for j in range(supernodes):
        at = slice(j * width, (j + 1) * width)
        rows = jnp.concatenate([a_ref[:, at], w_ref[:, at]], axis=0)
        copies[3 + j].wait()
        product = mm(rows, t_ref[j], HIGHEST)
        scale = structure_ref[j, place_ref[0]].astype(F32)
        a = (scale * product[:local]).astype(BF16)
        for copy in range(2):
            start = (copy * supernodes + j) * width
            panel_ref[:, start : start + width] = a
        h, off = divmod(j * width, ha)
        message_ref[h, :local, off : off + width] = a
        if j == 0:
            continue
        scale = jnp.where(place_ref[1] < j, 1.0, 0.0)
        w = (scale * product[local:]).astype(BF16)
        for half in range(2):
            message_ref[half, local:, (j - 1) * width // 2 : j * width // 2] = w[
                :, half * width // 2 : (half + 1) * width // 2
            ]


def pack_kernel(got_ref, out_ref):
    blocks, height, columns = got_ref.shape
    rows = (out_ref.shape[0] - 96) // blocks
    edge = rows * blocks
    half = columns // 4
    for i in range(blocks):
        out_ref[i * rows : (i + 1) * rows] = got_ref[i, :rows]
    for k in range(2):
        for c in range(2):
            at = edge + (2 * k + c) * 16
            block = 2 * k + c
            out_ref[at : at + 16, : 3 * half] = got_ref[block, rows:, : 3 * half]
            out_ref[at : at + 16, 3 * half :] = got_ref[8 + block, rows:, 2 * half : 3 * half]
            at = edge + 64 + c * 16
            out_ref[at : at + 16, 2 * k * half : 2 * (k + 1) * half] = got_ref[
                4 + block, rows:, half : 3 * half
            ]


def split(v):
    high = v.astype(BF16)
    return high, (v - high.astype(F32)).astype(BF16)


def dot(a, b):
    return jnp.dot(a, b, preferred_element_type=F32)


def dot_t(a, b):
    return lax.dot_general(a, b, (((0,), (0,)), ((), ())), preferred_element_type=F32)


def product_kernel(x_ref, sigma_ref, p0_ref, p1_ref, p2_ref, p3_ref, out_ref, held_ref):
    nz, nx, rows, columns = held_ref.shape
    for shift, ref in enumerate((p0_ref, p1_ref, p2_ref, p3_ref)):
        source = lax.rem(x_ref[0] + nx - shift, nx)
        for i in range(nz):
            held_ref[i, source] = ref[i * rows : (i + 1) * rows]
    out_ref[...] = dot(sigma_ref[...], held_ref[...].reshape(nz * nx * rows, columns))


def inverse_kernel(core_ref, x_ref, *refs):
    pieces, (high_ref, low_ref, held_ref) = refs[:8], refs[8:]
    width = high_ref.shape[0] // 3
    half = width // 2
    nx = held_ref.shape[3]
    edge = pieces[0].shape[0] - 96
    for group in range(2):
        side = core_ref[0] if group == 0 else 1 - core_ref[0]
        for shift in range(nx):
            ref = pieces[group * nx + shift]
            source = lax.rem(x_ref[0] + nx - shift, nx)
            for k in range(2):
                at = slice(edge + k * 32, edge + (k + 1) * 32)
                held_ref[side, 0, k, source] = ref[at, : 3 * half]
                held_ref[side, 1, k, source, :, half:] = ref[
                    edge + 64 : edge + 96, 2 * k * half : 2 * (k + 1) * half
                ]
                held_ref[side, 2, k, source, :, 2 * half :] = ref[at, 3 * half :]
    w = lambda i, j: jnp.concatenate(
        [
            held_ref[side, i, :, :, :, (j - 1) * half : j * half].reshape(width, half)
            for side in range(2)
        ],
        axis=1,
    )
    f = lambda i, j: w(i, j).astype(F32)
    u = {(i, i + 1): -f(i, i + 1) for i in range(3)}
    u[0, 2] = dot(w(0, 1), w(1, 2)) - f(0, 2)
    u[1, 3] = dot(w(1, 2), w(2, 3)) - f(1, 3)
    high, low = split(u[0, 2])
    u[0, 3] = dot(w(0, 1), w(1, 3)) - f(0, 3) - dot(high, w(2, 3)) - dot(low, w(2, 3))
    for i in range(3):
        for j in range(1, 4):
            at = (slice(i * width, (i + 1) * width), slice((j - 1) * width, j * width))
            value = u.get((i, j))
            value = jnp.zeros((width, width), F32) if value is None else value
            high_ref[at], low_ref[at] = split(value)


def left_kernel(panel_ref, high_ref, low_ref, lh_ref, ll_ref):
    width = lh_ref.shape[1] // 4
    lh_ref[:, :width] = panel_ref[:, :width]
    ll_ref[:, :width] = jnp.zeros((panel_ref.shape[0], width), BF16)
    for j in range(1, 4):
        a = panel_ref[:, : j * width]
        at = (slice(0, j * width), slice((j - 1) * width, j * width))
        value = panel_ref[:, j * width : (j + 1) * width].astype(F32)
        value = value + dot(a, high_ref[at]) + dot(a, low_ref[at])
        cut = slice(j * width, (j + 1) * width)
        lh_ref[:, cut], ll_ref[:, cut] = split(value)


def window_kernel(
    core_ref, structure_ref, z_ref, mine_ref, other_ref, high_ref, low_ref, lh_ref, ll_ref,
    right_ref, packed_ref, rh_ref, rl_ref, fh_ref, fl_ref,
):
    nc, nx, rows, _ = packed_ref.shape
    size, window = rh_ref.shape
    width = window // 4
    first = core_ref[0] == 0
    ny, local = right_ref.shape[0], right_ref.shape[1]
    fs = []
    for h in range(2):
        a, b = (mine_ref, other_ref) if h == 0 else (other_ref, mine_ref)
        value = jnp.where(first, a[...], b[...])
        at = slice(h * window // 2, (h + 1) * window // 2)
        fh_ref[:, at], fl_ref[:, at] = split(value)
        fs += [value[:, :width], value[:, width:]]
    for j in range(4):
        value = fs[j]
        if j:
            at = (slice(0, j * width), slice((j - 1) * width, j * width))
            fh = fh_ref[:, : j * width]
            value = value + (
                dot(fh, high_ref[at]) + dot(fl_ref[:, : j * width], high_ref[at]) + dot(fh, low_ref[at])
            )
        cut = slice(j * width, (j + 1) * width)
        for i in range(ny):
            select = structure_ref[j, i * ny + z_ref[0]].astype(F32)
            right_ref[i, :, cut] = -(select * value[i * local : (i + 1) * local])
        rh_ref[:, cut], rl_ref[:, cut] = split(value)
    at = 0
    for t in range(4):
        n = window - t * width
        cut = slice(t * width, (t + 1) * width)
        lh, ll = lh_ref[:, cut], ll_ref[:, cut]
        rh, rl = rh_ref[:, t * width :], rl_ref[:, t * width :]
        part = dot_t(lh, rh) + dot_t(ll, rh) + dot_t(lh, rl)
        for k in range(2):
            for i in range(nx):
                for c in range(nc):
                    row = ((k * nx + i) * nc + c) * rows
                    packed_ref[c, i, :, at : at + n] = part[row : row + rows]
            at += n


def exponent(v):
    top = jnp.max(jnp.abs(v), axis=(0, 1), keepdims=True)
    return jnp.floor(jnp.log2(jnp.maximum(top, 1e-30))) - 13.0


def sum_kernel(in_ref, out_ref):
    _, nx, rows, n = in_ref.shape
    for i in range(nx):
        total = in_ref[0, i] + in_ref[1, i]
        power = exponent(total)
        out_ref[i, :, :n] = total * jnp.exp2(-power)
        out_ref[i, :, n:] = jnp.broadcast_to(power, (rows, out_ref.shape[2] - n))


def spread_kernel(in_ref, out_ref):
    size, rows, window = out_ref.shape[0], out_ref.shape[1], out_ref.shape[2] - 128
    width = window // 4
    last = in_ref.shape[2] - 128
    scales = [jnp.exp2(in_ref[k, :, last : last + 1]) for k in range(in_ref.shape[0])]
    at = 0
    for i in range(size):
        edge = (i // 2) * width
        n = window - edge
        total = in_ref[0, :, at : at + n] * scales[0]
        for k in range(1, in_ref.shape[0]):
            total = total + in_ref[k, :, at : at + n] * scales[k]
        power = exponent(total)
        if edge:
            out_ref[i, :, :edge] = jnp.zeros((rows, edge), F32)
        out_ref[i, :, edge:window] = total * jnp.exp2(-power)
        out_ref[i, :, window:] = jnp.broadcast_to(power, (rows, 128))
        at += n


def repeat_kernel(in_ref, out_ref):
    window = out_ref.shape[1] - 128
    total = jnp.zeros((out_ref.shape[0], window), F32)
    for i in range(in_ref.shape[0]):
        total = total + in_ref[i, :, :window] * jnp.exp2(in_ref[i, :, window : window + 1])
    power = exponent(total)
    out_ref[:, :window] = total * jnp.exp2(-power)
    out_ref[:, window:] = jnp.broadcast_to(power, (out_ref.shape[0], 128))


def finish_kernel(tile_ref, in_ref, base_ref, out_ref):
    total = base_ref[...]
    window = total.shape[1]
    for i in range(in_ref.shape[0]):
        total = total + in_ref[i, :, :window] * jnp.exp2(in_ref[i, :, window : window + 1])
    columns = lax.broadcasted_iota(jnp.int32, total.shape, 1)
    out_ref[...] = jnp.where(columns >= tile_ref[0] * (window // 4), total, 0.0)


def base_kernel(place_ref, t_ref, high_ref, low_ref, out_ref, vh_ref, vl_ref, rows_ref):
    n, width = t_ref.shape[0], t_ref.shape[1]
    for k in range(n):
        th, tl = split(t_ref[k])
        down = slice(k * width, (k + 1) * width)
        for j in range(n):
            if j < k:
                zero = jnp.zeros((width, width), BF16)
                vh_ref[j, down], vl_ref[j, down] = zero, zero
            elif j == k:
                vh_ref[j, down], vl_ref[j, down] = th, tl
            else:
                at = (down, slice((j - 1) * width, j * width))
                value = dot(th, high_ref[at]) + dot(tl, high_ref[at]) + dot(th, low_ref[at])
                vh_ref[j, down], vl_ref[j, down] = split(value)
    ah, al = vh_ref[place_ref[1]], vl_ref[place_ref[1]]
    for j in range(n):
        vh, vl = vh_ref[j], vl_ref[j]
        rows_ref[:, j * width : (j + 1) * width] = dot_t(ah, vh) + dot_t(al, vh) + dot_t(ah, vl)
    rows = out_ref.shape[0]
    out_ref[...] = rows_ref[pl.ds(pl.multiple_of(place_ref[2] * rows, rows), rows)]


def body(sigma_top, ancestor_rows, window_rows, tile_inverse, structure):
    ny, nz, nx, nc = 8, 8, 4, 2
    supernodes, width = tile_inverse.shape[0], tile_inverse.shape[1]
    window = supernodes * width
    local = ancestor_rows.shape[0]
    wlocal = window_rows.shape[0]
    y, z, x, c = (lax.axis_index(name) for name in ("y", "z", "x", "c"))
    col = (z * nx + x) * nc + c
    tile = ((y * (nz * nx * nc) + col) * local) // width
    wtile = (col * wlocal) // width

    with jax.named_scope("panels"):
        ha, hw = window // 2, (window - width) // 2
        place = jnp.stack([tile, wtile, col % (width // wlocal)])
        message, panel = local_call(
            panel_kernel,
            (
                jax.ShapeDtypeStruct((nc, local + wlocal, ha), BF16),
                jax.ShapeDtypeStruct((local, 2 * window), BF16),
            ),
            (place,),
            structure,
            ancestor_rows,
            window_rows,
            tile_inverse,
            scratch=(
                pltpu.SMEM(structure.shape, jnp.int32),
                (ancestor_rows.shape, F32),
                (window_rows.shape, F32),
                (tile_inverse.shape, F32),
                pltpu.SemaphoreType.DMA((3 + supernodes,)),
            ),
            far=True,
            mebibytes=56,
        )

    shape = lambda *dims, dtype=F32: jax.ShapeDtypeStruct(dims, dtype)
    with jax.named_scope("column_block"):
        panel_c = lax.all_gather(panel, "y", axis=0, tiled=True)

    with jax.named_scope("gather"):
        got = exchange(message, "c").reshape(nc, local + wlocal, ha)
        got = lax.all_gather(got, "z", axis=0, tiled=True)
        swap = [(0, 1), (1, 0)]
        first = local_call(
            pack_kernel, shape(nz * nc * local + 96, ha, dtype=BF16), (), got
        )
        pieces = [first]
        for step in range(1, nx):
            pieces.append(
                lax.ppermute(first, "x", [(i, (i + step) % nx) for i in range(nx)])
            )
        others = [lax.ppermute(piece, "c", swap) for piece in pieces]

    with jax.named_scope("unit_inverse"):
        core = c.reshape(1)
        n = window - width
        high, low = local_call(
            inverse_kernel,
            (shape(n, n, dtype=BF16), shape(n, n, dtype=BF16)),
            (core, x.reshape(1)),
            *pieces,
            *others,
            scratch=(((2, supernodes - 1, 2, nx, 2 * wlocal, n // 2), BF16),),
        )
        lh, ll = local_call(
            left_kernel,
            (shape(ny * local, window, dtype=BF16),) * 2,
            (),
            panel_c,
            high,
            low,
        )

    with jax.named_scope("product"):
        sigma = sigma_top.transpose(1, 2, 3, 0).reshape(ny * local, -1)
        held = (((nz, nx, nc * local, ha), BF16),)
        product = lambda parts: local_call(
            product_kernel,
            shape(ny * local, ha),
            (x.reshape(1),),
            sigma,
            *parts,
            scratch=held,
        )
        own = product(pieces)
        away = product(others)

    with jax.named_scope("window"):
        half = ((ny * local, window), BF16)
        packed = (nx, wlocal, 2 * 10 * width)
        right, packed_sum = local_call(
            window_kernel,
            (shape(ny, local, window), shape(nc, *packed)),
            (core, structure, z.reshape(1)),
            own,
            away,
            high,
            low,
            lh,
            ll,
            scratch=(half, half, half, half),
        )
        cross = lax.psum_scatter(right, "y", scatter_dimension=0, tiled=True)
        cross = cross.reshape(local, window)
        packed_sum = exchange(packed_sum, "c").reshape(nc, *packed)
        half_type = jnp.float16
        n = packed[-1] + 128
        parts = local_call(sum_kernel, shape(nx, wlocal, n), (), packed_sum)
        parts = exchange(parts.astype(half_type), "x").astype(F32)
        spread = local_call(spread_kernel, shape(nz, wlocal, window + 128), (), parts)
        spread = exchange(spread.astype(half_type), "z").astype(F32)
        spread = local_call(repeat_kernel, shape(wlocal, window + 128), (), spread)
        spread = gather(spread.astype(half_type), "y", ny).astype(F32)

    with jax.named_scope("diagonal"):
        spare = ((supernodes, window, width), BF16)
        base = local_call(
            base_kernel,
            shape(wlocal, window),
            (place,),
            tile_inverse,
            high,
            low,
            scratch=(spare, spare, ((width, window), F32)),
        )
        block = local_call(
            finish_kernel, shape(wlocal, window), (wtile.reshape(1),), spread, base
        )
    return cross, block


def solution(mesh):
    fine = Mesh(mesh.devices.reshape(8, 8, 4, 2), ("y", "z", "x", "c"))
    col = ("z", "x", "c")
    return jax.shard_map(
        body,
        mesh=fine,
        in_specs=(P("y", None, col, None), P(("y",) + col, None), P(col, None), P(), P()),
        out_specs=(P(("y",) + col, None), P(col, None)),
        check_vma=False,
    )
```
